32 devices in a mesh: seq: 8 (over z, x), fsdp: 4 (over y, core).
Axes of the slice: x: 2, y: 2, z: 4, core: 2. Of those that a mesh axis runs over, the one named last changes fastest.
Arguments:
- query_rows: bfloat16 [4096, 4096], P('seq', 'fsdp'), may hold values from -6 to 6
- key_rows: bfloat16 [4096, 4096], P('seq', 'fsdp'), may hold values from -0.5390625 to 0.5390625
- value_rows: bfloat16 [4096, 4096], P('seq', 'fsdp'), may hold values from -6 to 6
- norm_gain: float32 [4096], P('fsdp'), may hold values from 0.1 to 1.9
- out_weight: bfloat16 [4096, 4096], P(None, 'fsdp'), may hold values from -0.09375 to 0.09375
Outputs:
- mixed: bfloat16 [4096, 4096], P('seq', 'fsdp')
The draws below stay inside these ranges and needn't reach their ends.
All inputs are finite; a program needn't handle non-finite values.
Results may differ from the reference program's by a relative error of at most 0.012.
Values may be sent and summed in bfloat16 or wider, within the bound.
A program may use at most 192 MiB of HBM per device.

```python
import jax
import jax.numpy as jnp
from jax import lax

D = 4096
HEADS = 32
DH = 128
BLK = 512
TOKENS = 4096


def block_levels(stream_key, dims, pieces, least, largest):
    def one(axis_at, parts):
        heights = jax.random.uniform(jax.random.fold_in(jax.random.fold_in(stream_key, 6), axis_at), (parts,), jnp.float32, least / len(pieces), largest / len(pieces))
        return jnp.repeat(jnp.exp(heights), dims[axis_at] // parts).reshape((-1,) + (1,) * (len(dims) - axis_at - 1))

    loudness = one(*pieces[0])
    for cut in pieces[1:]:
        loudness = loudness * one(*cut)
    return loudness


def noise(key, dims, width, limit, cuts=(), kind=jnp.bfloat16):
    loudness = block_levels(key, dims, cuts, -0.22, 0.18) if cuts else 1.0
    result = jax.random.normal(key, dims, jnp.float32) * width * loudness
    return jnp.minimum(jnp.maximum(result, -limit), limit).astype(kind)


def setup_inputs(seed: int = 0) -> dict:
    streams_of = jax.random.split(jax.random.key(seed), 6)
    return {
        "query_rows": noise(streams_of[0], (TOKENS, HEADS * DH), 1.0, 6.0, ((0, 8), (1, 4))),
        "key_rows": noise(streams_of[1], (TOKENS, HEADS * DH), 0.09, 0.5390625, ((0, 8), (1, 4))),
        "value_rows": noise(streams_of[2], (TOKENS, HEADS * DH), 1.0, 6.0, ((0, 8), (1, 4))),
        "norm_gain": jnp.clip(1.0 + 0.18 * jax.random.normal(streams_of[3], (HEADS * DH,), jnp.float32), 0.1, 1.9),
        "out_weight": noise(streams_of[4], (HEADS * DH, D), (HEADS * DH) ** -0.5, 0.09375, ((1, 4),)),
    }


def reference(query_rows, key_rows, value_rows, norm_gain, out_weight):
    n_blocks = TOKENS // BLK
    queries_b = query_rows.reshape(n_blocks, BLK, HEADS, DH).astype(jnp.float32)
    keys_b = key_rows.reshape(n_blocks, BLK, HEADS, DH).astype(jnp.float32)
    values_b = value_rows.reshape(n_blocks, BLK, HEADS, DH).astype(jnp.float32)
    position = lax.broadcasted_iota(jnp.int32, (BLK, BLK), 0)
    column = lax.broadcasted_iota(jnp.int32, (BLK, BLK), 1)
    causal_mask = column <= position
    highest = lax.Precision.HIGHEST

    def block_step(carried, block_data):
        query_block, key_block, value_block = block_data
        scores = jnp.einsum('qhd,khd->hqk', query_block, key_block, precision=highest)
        masked_scores = jnp.where(causal_mask[None], scores, 0.0).astype(jnp.bfloat16)
        within_block = jnp.einsum('hqk,khd->qhd', masked_scores.astype(jnp.float32), value_block, precision=highest)
        from_state = jnp.einsum('qhd,hde->qhe', query_block, carried, precision=highest)
        block_state = jnp.einsum('khd,khe->hde', key_block, value_block, precision=highest)
        return (carried + block_state, within_block + from_state)
    start_state = jnp.zeros((HEADS, DH, DH), jnp.float32)
    final_state, attention = lax.scan(block_step, start_state, (queries_b, keys_b, values_b))
    mean_square = lax.optimization_barrier(jnp.mean(attention * attention, axis=-1, keepdims=True))
    normed = attention * lax.rsqrt(mean_square + 1e-06) * norm_gain.reshape(HEADS, DH)
    normed = normed.astype(jnp.bfloat16).reshape(TOKENS, HEADS * DH)
    return jnp.dot(normed, out_weight, preferred_element_type=jnp.float32).astype(jnp.bfloat16)
```

```python
import functools

import jax
import jax.numpy as jnp
from jax import lax
from jax.experimental import pallas as pl
from jax.experimental.pallas import tpu as pltpu
from jax.sharding import PartitionSpec as P

DH = 128
TILE = 256
AHEAD = 2
MESH = pl.DeviceIdType.MESH
F32 = jnp.float32
BF16 = jnp.bfloat16


def dot(a, b, contract=((1,), (0,))):
    return lax.dot_general(a, b, (contract, ((), ())), preferred_element_type=F32)


def kernel(
    seq_n, q_hbm, k_hbm, v_hbm, gain_ref, w_hbm, o_ref,
    q, k, v, w, g, state, s_send, x_recv, c_send, c_recv, carry, within, acc,
    load_sem, w_sem, xs, xr, cs, cr, ss, sr, ys, yr, fs, fr,
):
    tokens, width = q.shape
    heads = width // DH
    i, f = lax.axis_index("seq"), lax.axis_index("fsdp")
    odd = lax.rem(i, 2)
    pair = i + 1 - 2 * odd
    sibling = f + 1 - 2 * lax.rem(f, 2)
    across = lax.rem(f + 2, 4)
    has_before = i >= 2
    has_after = i < seq_n - 2

    loads = [
        pltpu.make_async_copy(src, dst, load_sem.at[n])
        for n, (src, dst) in enumerate(((k_hbm, k), (v_hbm, v), (q_hbm, q)))
    ]
    for load in loads:
        load.start()
    w_loads = []
    for slot, source in enumerate((f, sibling, across, 3 - f)):
        rows = pl.ds(pl.multiple_of(source * width, width), width)
        w_loads.append(pltpu.make_async_copy(w_hbm.at[rows], w.at[slot], w_sem.at[slot]))

    barrier = pltpu.get_barrier_semaphore()

    def greet(j, e):
        pl.semaphore_signal(barrier, inc=1, device_id=(j, e), device_id_type=MESH)

    greet(pair, f)
    greet(i, sibling)
    greet(i, across)

    @pl.when(has_before)
    def _():
        greet(i - 2, f)

    @pl.when(has_after)
    def _():
        greet(i + 2, f)

    pl.semaphore_wait(barrier, 3 + has_before.astype(jnp.int32) + has_after.astype(jnp.int32))

    def remote(src, dst, send, recv, h, where):
        return pltpu.make_async_remote_copy(
            src_ref=src.at[h], dst_ref=dst.at[h], send_sem=send.at[h], recv_sem=recv.at[h],
            device_id=where, device_id_type=MESH,
        )

    after = lax.rem(i + 2, seq_n)
    to_pair = lambda h: remote(s_send, x_recv, xs, xr, h, (pair, f))
    to_after = lambda h: remote(c_send, c_recv, cs, cr, h, (after, f))
    to_sibling = lambda h: remote(g.at[0], g.at[1], ss, sr, h, (i, sibling))
    to_across = lambda h: remote(g.at[0], g.at[2], ys, yr, h, (i, across))
    pass_on = lambda h: remote(g.at[2], g.at[3], fs, fr, h, (i, sibling))

    loads[0].wait()
    loads[1].wait()
    for h in range(heads):
        columns = slice(h * DH, (h + 1) * DH)
        s = dot(k[:, columns], v[:, columns], ((0,), (0,)))
        state[h] = s
        s_send[h] = s.astype(BF16)
        to_pair(h).start()
    for load in w_loads:
        load.start()
    loads[2].wait()

    def head_step(h, _):
        columns = pl.ds(pl.multiple_of(h * DH, DH), DH)
        for r in range(tokens // TILE):
            rows = slice(r * TILE, (r + 1) * TILE)
            scores = dot(q[rows, columns], k[: (r + 1) * TILE, columns], ((1,), (1,)))
            row = lax.broadcasted_iota(jnp.int32, scores.shape, 0) + r * TILE
            column = lax.broadcasted_iota(jnp.int32, scores.shape, 1)
            masked = jnp.where(column <= row, scores, 0.0).astype(BF16)
            within[rows] = dot(masked, v[: (r + 1) * TILE, columns])

        to_pair(h).wait_recv()
        other = x_recv[h].astype(F32)
        total = state[h] + other
        mine = jnp.where(odd == 1, other, 0.0)

        @pl.when(has_before)
        def _():
            to_after(h).wait_recv()

            @pl.when(has_after)
            def _():
                c_send[h] = (total + c_recv[h].astype(F32)).astype(BF16)

            carry[...] = (mine + c_recv[h].astype(F32)).astype(BF16)

        @pl.when(jnp.logical_not(has_before))
        def _():
            c_send[h] = total.astype(BF16)
            carry[...] = mine.astype(BF16)

        @pl.when(has_after)
        def _():
            to_after(h).start()

        attention = within[...] + dot(q[:, columns], carry[...])
        mean_square = jnp.mean(attention * attention, axis=-1, keepdims=True)
        normed = attention * lax.rsqrt(mean_square + 1e-06) * gain_ref[:, columns]
        g[0, h] = normed.astype(BF16)
        to_sibling(h).start()

        @pl.when(h < AHEAD)
        def _():
            to_across(h).start()

        return 0

    lax.fori_loop(0, heads, head_step, 0)

    def whole_slot(slot, fresh):
        for n in range(0, acc.shape[1], TILE):
            columns = slice(n, n + TILE)
            part = None if fresh else acc[:, columns]
            for h in range(0, heads, 2):
                lhs = jnp.concatenate([g[slot, h], g[slot, h + 1]], axis=1)
                new = dot(lhs, w[slot, h * DH : (h + 2) * DH, columns])
                part = new if part is None else part + new
            acc[:, columns] = part

    w_loads[0].wait()
    whole_slot(0, True)
    w_loads[1].wait()

    def sibling_step(h, _):
        to_sibling(h).wait_recv()
        return 0

    lax.fori_loop(0, heads, sibling_step, 0)
    whole_slot(1, False)
    w_loads[2].wait()
    w_loads[3].wait()

    def arrive(h):
        to_across(h).wait_recv()
        pass_on(h).start()

        @pl.when(h + AHEAD < heads)
        def _():
            to_across(h).wait_send()
            to_across(h + AHEAD).start()

    def rows_of(slot, h):
        return w[slot, pl.ds(pl.multiple_of(h * DH, DH), DH)]

    arrive(jnp.int32(0))
    acc[...] += dot(g[2, 0], w[2, :DH])

    def across_step(h, _):
        arrive(h)
        pass_on(h - 1).wait_recv()
        lhs = jnp.concatenate([g[2, h], g[3, h - 1]], axis=1)
        rhs = jnp.concatenate([rows_of(2, h), rows_of(3, h - 1)], axis=0)
        acc[...] += dot(lhs, rhs)
        return 0

    lax.fori_loop(1, heads, across_step, 0)
    pass_on(heads - 1).wait_recv()
    last = dot(g[3, heads - 1], w[3, (heads - 1) * DH :])
    o_ref[...] = (acc[...] + last).astype(BF16)

    def drain(h, _):
        to_pair(h).wait_send()
        to_sibling(h).wait_send()
        pass_on(h).wait_send()

        @pl.when(h + AHEAD >= heads)
        def _():
            to_across(h).wait_send()

        @pl.when(has_after)
        def _():
            to_after(h).wait_send()

        return 0

    lax.fori_loop(0, heads, drain, 0)


def shards(seq_n, query_rows, key_rows, value_rows, norm_gain, out_weight):
    tokens, width = query_rows.shape
    heads = width // DH
    features = out_weight.shape[1]
    hbm = pl.BlockSpec(memory_space=pl.ANY)
    vmem = pl.BlockSpec(memory_space=pltpu.VMEM)
    small = (heads, DH, DH)
    return pl.pallas_call(
        functools.partial(kernel, seq_n),
        out_shape=jax.ShapeDtypeStruct((tokens, features), BF16),
        in_specs=[hbm, hbm, hbm, vmem, hbm],
        out_specs=vmem,
        scratch_shapes=[
            pltpu.VMEM((tokens, width), BF16),
            pltpu.VMEM((tokens, width), BF16),
            pltpu.VMEM((tokens, width), BF16),
            pltpu.VMEM((4, width, features), BF16),
            pltpu.VMEM((4, heads, tokens, DH), BF16),
            pltpu.VMEM(small, F32),
            pltpu.VMEM(small, BF16),
            pltpu.VMEM(small, BF16),
            pltpu.VMEM(small, BF16),
            pltpu.VMEM(small, BF16),
            pltpu.VMEM((DH, DH), BF16),
            pltpu.VMEM((tokens, DH), F32),
            pltpu.VMEM((tokens, features), F32),
            pltpu.SemaphoreType.DMA((3,)),
            pltpu.SemaphoreType.DMA((4,)),
        ]
        + [pltpu.SemaphoreType.DMA((heads,))] * 10,
        compiler_params=pltpu.CompilerParams(
            collective_id=0, has_side_effects=True, vmem_limit_bytes=48 * 1024 * 1024
        ),
        cost_estimate=pl.CostEstimate(
            flops=2 * tokens * width * 4 * features + 6 * tokens * tokens * width,
            bytes_accessed=2 * (4 * tokens * width + 4 * width * features),
            transcendentals=tokens * heads,
        ),
    )(query_rows, key_rows, value_rows, norm_gain.reshape(1, -1), out_weight)


def solution(mesh):
    placed = (P("seq", "fsdp"), P("seq", "fsdp"), P("seq", "fsdp"), P("fsdp"), P(None, "fsdp"))
    return jax.shard_map(
        functools.partial(shards, mesh.shape["seq"]),
        mesh=mesh, in_specs=placed, out_specs=P("seq", "fsdp"), check_vma=False,
    )
```

```python
import functools

import jax
import jax.numpy as jnp
from jax import lax
from jax.experimental import pallas as pl
from jax.experimental.pallas import tpu as pltpu
from jax.sharding import PartitionSpec as P

DH = 128
TILE = 256
AHEAD = 4
MESH = pl.DeviceIdType.MESH
F32 = jnp.float32
BF16 = jnp.bfloat16


def dot(a, b, contract=((1,), (0,))):
    return lax.dot_general(a, b, (contract, ((), ())), preferred_element_type=F32)


def kernel(
    seq_n, q_hbm, k_hbm, v_hbm, gain_ref, w_hbm, o_ref,
    q, k, v, w, g, state, s_send, x_recv, c_send, c_recv, carry, within, acc,
    load_sem, w_sem, xs, xr, cs, cr, ss, sr, ys, yr, fs, fr,
):
    tokens, width = q.shape
    heads = width // DH
    i, f = lax.axis_index("seq"), lax.axis_index("fsdp")
    odd = lax.rem(i, 2)
    pair = i + 1 - 2 * odd
    sibling = f + 1 - 2 * lax.rem(f, 2)
    across = lax.rem(f + 2, 4)
    has_before = i >= 2
    has_after = i < seq_n - 2

    loads = [
        pltpu.make_async_copy(src, dst, load_sem.at[n])
        for n, (src, dst) in enumerate(((k_hbm, k), (v_hbm, v), (q_hbm, q)))
    ]
    for load in loads:
        load.start()
    w_loads = []
    for slot, source in enumerate((f, sibling, across, 3 - f)):
        rows = pl.ds(pl.multiple_of(source * width, width), width)
        w_loads.append(pltpu.make_async_copy(w_hbm.at[rows], w.at[slot], w_sem.at[slot]))

    barrier = pltpu.get_barrier_semaphore()

    def greet(j, e):
        pl.semaphore_signal(barrier, inc=1, device_id=(j, e), device_id_type=MESH)

    greet(pair, f)
    greet(i, sibling)
    greet(i, across)

    @pl.when(has_before)
    def _():
        greet(i - 2, f)

    @pl.when(has_after)
    def _():
        greet(i + 2, f)

    pl.semaphore_wait(barrier, 3 + has_before.astype(jnp.int32) + has_after.astype(jnp.int32))

    def remote(src, dst, send, recv, h, where):
        return pltpu.make_async_remote_copy(
            src_ref=src.at[h], dst_ref=dst.at[h], send_sem=send.at[h], recv_sem=recv.at[h],
            device_id=where, device_id_type=MESH,
        )

    after = lax.rem(i + 2, seq_n)
    to_pair = lambda h: remote(s_send, x_recv, xs, xr, h, (pair, f))
    to_after = lambda h: remote(c_send, c_recv, cs, cr, h, (after, f))
    to_sibling = lambda h: remote(g.at[0], g.at[1], ss, sr, h, (i, sibling))
    to_across = lambda h: remote(g.at[0], g.at[2], ys, yr, h, (i, across))
    pass_on = lambda h: remote(g.at[2], g.at[3], fs, fr, h, (i, sibling))

    loads[0].wait()
    loads[1].wait()
    for h in range(heads):
        columns = slice(h * DH, (h + 1) * DH)
        s = dot(k[:, columns], v[:, columns], ((0,), (0,)))
        state[h] = s
        s_send[h] = s.astype(BF16)
        to_pair(h).start()
    for load in w_loads:
        load.start()
    loads[2].wait()

    def head_step(h, _):
        columns = pl.ds(pl.multiple_of(h * DH, DH), DH)
        for r in range(tokens // TILE):
            rows = slice(r * TILE, (r + 1) * TILE)
            scores = dot(q[rows, columns], k[: (r + 1) * TILE, columns], ((1,), (1,)))
            row = lax.broadcasted_iota(jnp.int32, scores.shape, 0) + r * TILE
            column = lax.broadcasted_iota(jnp.int32, scores.shape, 1)
            masked = jnp.where(column <= row, scores, 0.0).astype(BF16)
            within[rows] = dot(masked, v[: (r + 1) * TILE, columns])

        to_pair(h).wait_recv()
        other = x_recv[h].astype(F32)
        total = state[h] + other
        mine = jnp.where(odd == 1, other, 0.0)

        @pl.when(has_before)
        def _():
            to_after(h).wait_recv()

            @pl.when(has_after)
            def _():
                c_send[h] = (total + c_recv[h].astype(F32)).astype(BF16)

            carry[...] = (mine + c_recv[h].astype(F32)).astype(BF16)

        @pl.when(jnp.logical_not(has_before))
        def _():
            c_send[h] = total.astype(BF16)
            carry[...] = mine.astype(BF16)

        @pl.when(has_after)
        def _():
            to_after(h).start()

        attention = within[...] + dot(q[:, columns], carry[...])
        mean_square = jnp.mean(attention * attention, axis=-1, keepdims=True)
        normed = attention * lax.rsqrt(mean_square + 1e-06) * gain_ref[:, columns]
        g[0, h] = normed.astype(BF16)
        to_sibling(h).start()

        @pl.when(h < AHEAD)
        def _():
            to_across(h).start()

        return 0

    lax.fori_loop(0, heads, head_step, 0)

    def whole_slot(slot, fresh):
        for n in range(0, acc.shape[1], TILE):
            columns = slice(n, n + TILE)
            part = None if fresh else acc[:, columns]
            for h in range(0, heads, 2):
                lhs = jnp.concatenate([g[slot, h], g[slot, h + 1]], axis=1)
                new = dot(lhs, w[slot, h * DH : (h + 2) * DH, columns])
                part = new if part is None else part + new
            acc[:, columns] = part

    w_loads[0].wait()
    whole_slot(0, True)
    w_loads[1].wait()

    def sibling_step(h, _):
        to_sibling(h).wait_recv()
        return 0

    lax.fori_loop(0, heads, sibling_step, 0)
    whole_slot(1, False)
    w_loads[2].wait()
    w_loads[3].wait()

    def arrive(h):
        to_across(h).wait_recv()
        pass_on(h).start()

        @pl.when(h + AHEAD < heads)
        def _():
            to_across(h).wait_send()
            to_across(h + AHEAD).start()

    def rows_of(slot, h):
        return w[slot, pl.ds(pl.multiple_of(h * DH, DH), DH)]

    arrive(jnp.int32(0))
    acc[...] += dot(g[2, 0], w[2, :DH])

    def across_step(h, _):
        arrive(h)
        pass_on(h - 1).wait_recv()
        lhs = jnp.concatenate([g[2, h], g[3, h - 1]], axis=1)
        rhs = jnp.concatenate([rows_of(2, h), rows_of(3, h - 1)], axis=0)
        acc[...] += dot(lhs, rhs)
        return 0

    lax.fori_loop(1, heads, across_step, 0)
    pass_on(heads - 1).wait_recv()
    last = dot(g[3, heads - 1], w[3, (heads - 1) * DH :])
    o_ref[...] = (acc[...] + last).astype(BF16)

    def drain(h, _):
        to_pair(h).wait_send()
        to_sibling(h).wait_send()
        pass_on(h).wait_send()

        @pl.when(h + AHEAD >= heads)
        def _():
            to_across(h).wait_send()

        @pl.when(has_after)
        def _():
            to_after(h).wait_send()

        return 0

    lax.fori_loop(0, heads, drain, 0)


def shards(seq_n, query_rows, key_rows, value_rows, norm_gain, out_weight):
    tokens, width = query_rows.shape
    heads = width // DH
    features = out_weight.shape[1]
    hbm = pl.BlockSpec(memory_space=pl.ANY)
    vmem = pl.BlockSpec(memory_space=pltpu.VMEM)
    small = (heads, DH, DH)
    return pl.pallas_call(
        functools.partial(kernel, seq_n),
        out_shape=jax.ShapeDtypeStruct((tokens, features), BF16),
        in_specs=[hbm, hbm, hbm, vmem, hbm],
        out_specs=vmem,
        scratch_shapes=[
            pltpu.VMEM((tokens, width), BF16),
            pltpu.VMEM((tokens, width), BF16),
            pltpu.VMEM((tokens, width), BF16),
            pltpu.VMEM((4, width, features), BF16),
            pltpu.VMEM((4, heads, tokens, DH), BF16),
            pltpu.VMEM(small, F32),
            pltpu.VMEM(small, BF16),
            pltpu.VMEM(small, BF16),
            pltpu.VMEM(small, BF16),
            pltpu.VMEM(small, BF16),
            pltpu.VMEM((DH, DH), BF16),
            pltpu.VMEM((tokens, DH), F32),
            pltpu.VMEM((tokens, features), F32),
            pltpu.SemaphoreType.DMA((3,)),
            pltpu.SemaphoreType.DMA((4,)),
        ]
        + [pltpu.SemaphoreType.DMA((heads,))] * 10,
        compiler_params=pltpu.CompilerParams(
            collective_id=0, has_side_effects=True, vmem_limit_bytes=62 * 1024 * 1024
        ),
        cost_estimate=pl.CostEstimate(
            flops=2 * tokens * width * 4 * features + 6 * tokens * tokens * width,
            bytes_accessed=2 * (4 * tokens * width + 4 * width * features),
            transcendentals=tokens * heads,
        ),
    )(query_rows, key_rows, value_rows, norm_gain.reshape(1, -1), out_weight)


def solution(mesh):
    placed = (P("seq", "fsdp"), P("seq", "fsdp"), P("seq", "fsdp"), P("fsdp"), P(None, "fsdp"))
    return jax.shard_map(
        functools.partial(shards, mesh.shape["seq"]),
        mesh=mesh, in_specs=placed, out_specs=P("seq", "fsdp"), check_vma=False,
    )
```

```python
import functools

import jax
import jax.numpy as jnp
from jax import lax
from jax.experimental import pallas as pl
from jax.experimental.pallas import tpu as pltpu
from jax.sharding import PartitionSpec as P

DH = 128
TILE = 256
AHEAD = 4
EARLY = 3
MESH = pl.DeviceIdType.MESH
F32 = jnp.float32
BF16 = jnp.bfloat16


def dot(a, b, contract=((1,), (0,))):
    return lax.dot_general(a, b, (contract, ((), ())), preferred_element_type=F32)


def kernel(
    seq_n, q_hbm, k_hbm, v_hbm, gain_hbm, w_hbm, o_ref,
    q, k, v, w, g, state, s_send, x_recv, c_send, c_recv, carry, within, acc,
    gain, far_gain, far_q, far_within, far_carry, within_send,
    load_sem, w_sem, gain_sem, xs, xr, cs, cr, ss, sr, ys, yr, fs, fr, qs, qr, ws, wr,
):
    tokens, width = q.shape
    heads = width // DH
    i, f = lax.axis_index("seq"), lax.axis_index("fsdp")
    odd = lax.rem(i, 2)
    pair = i + 1 - 2 * odd
    sibling = f + 1 - 2 * lax.rem(f, 2)
    across = lax.rem(f + 2, 4)
    has_before = i >= 2
    has_after = i < seq_n - 2

    early = jnp.minimum(i // 2, min(EARLY, heads // 2))
    plain = heads - early
    first, rest = pl.ds(0, 2 * DH), pl.ds(2 * DH, width - 2 * DH)
    pieces = (
        (k_hbm.at[:, first], k.at[:, first]), (v_hbm.at[:, first], v.at[:, first]),
        (k_hbm.at[:, rest], k.at[:, rest]), (v_hbm.at[:, rest], v.at[:, rest]),
        (q_hbm, q), (gain_hbm, gain),
    )
    loads = [pltpu.make_async_copy(src, dst, load_sem.at[n]) for n, (src, dst) in enumerate(pieces)]
    for load in loads:
        load.start()
    w_loads = []
    for slot, source in enumerate((f, sibling, across, 3 - f)):
        rows = pl.ds(pl.multiple_of(source * width, width), width)
        w_loads.append(pltpu.make_async_copy(w_hbm.at[rows], w.at[slot], w_sem.at[slot]))

    barrier = pltpu.get_barrier_semaphore()

    def greet(j, e):
        pl.semaphore_signal(barrier, inc=1, device_id=(j, e), device_id_type=MESH)

    greet(pair, f)
    greet(i, sibling)
    greet(i, across)

    @pl.when(has_before)
    def _():
        greet(i - 2, f)

    @pl.when(has_after)
    def _():
        greet(i + 2, f)

    pl.semaphore_wait(barrier, 3 + has_before.astype(jnp.int32) + has_after.astype(jnp.int32))

    def remote(src, dst, send, recv, h, where):
        return pltpu.make_async_remote_copy(
            src_ref=src.at[h], dst_ref=dst.at[h], send_sem=send.at[h], recv_sem=recv.at[h],
            device_id=where, device_id_type=MESH,
        )

    after = lax.rem(i + 2, seq_n)
    to_pair = lambda h: remote(s_send, x_recv, xs, xr, h, (pair, f))
    to_after = lambda h: remote(c_send, c_recv, cs, cr, h, (after, f))
    to_sibling = lambda h: remote(g.at[0], g.at[1], ss, sr, h, (i, sibling))
    to_across = lambda h: remote(g.at[0], g.at[2], ys, yr, h, (i, across))
    pass_on = lambda h: remote(g.at[2], g.at[3], fs, fr, h, (i, sibling))

    far = (i, across)

    def across_copy(src, dst, send, recv):
        return pltpu.make_async_remote_copy(
            src_ref=src, dst_ref=dst, send_sem=send, recv_sem=recv, device_id=far, device_id_type=MESH
        )

    def columns_of(h):
        return pl.ds(pl.multiple_of(h * DH, DH), DH)

    gain_across = lambda: across_copy(gain_hbm, far_gain, gain_sem.at[0], gain_sem.at[1])

    def q_across(h):
        n = h - (heads - EARLY)
        return across_copy(q_hbm.at[:, columns_of(h)], far_q.at[n], qs.at[n], qr.at[n])

    def within_across(h):
        n = h - (heads - EARLY)
        return across_copy(within_send.at[n], far_within.at[n], ws.at[n], wr.at[n])

    def carry_across(h):
        return across_copy(carry.at[h], far_carry.at[h - (heads - EARLY)], ys.at[h], yr.at[h])

    def start_early(h, _):
        q_across(h).start()
        return 0

    loads[0].wait()
    loads[1].wait()
    for h in range(heads):
        if h == 2:
            loads[2].wait()
            loads[3].wait()
        columns = slice(h * DH, (h + 1) * DH)
        s = dot(k[:, columns], v[:, columns], ((0,), (0,)))
        state[h] = s
        s_send[h] = s.astype(BF16)
        to_pair(h).start()
        if h == 0:
            gain_across().start()
            lax.fori_loop(plain, heads, start_early, 0)
    for load in w_loads:
        load.start()
    loads[4].wait()
    loads[5].wait()

    def form_within(h):
        columns = columns_of(h)
        for r in range(tokens // TILE):
            rows = slice(r * TILE, (r + 1) * TILE)
            scores = dot(q[rows, columns], k[: (r + 1) * TILE, columns], ((1,), (1,)))
            row = lax.broadcasted_iota(jnp.int32, scores.shape, 0) + r * TILE
            column = lax.broadcasted_iota(jnp.int32, scores.shape, 1)
            masked = jnp.where(column <= row, scores, 0.0).astype(BF16)
            within[rows] = dot(masked, v[: (r + 1) * TILE, columns])

    def early_step(h, _):
        form_within(h)
        within_send[h - (heads - EARLY)] = within[...].astype(BF16)
        within_across(h).start()
        return 0

    lax.fori_loop(plain, heads, early_step, 0)

    def normalize(attention, gains):
        mean_square = jnp.mean(attention * attention, axis=-1, keepdims=True)
        return (attention * lax.rsqrt(mean_square + 1e-06) * gains).astype(BF16)

    def head_step(h, _):
        columns = columns_of(h)
        form_within(h)
        to_pair(h).wait_recv()
        other = x_recv[h].astype(F32)
        total = state[h] + other
        mine = jnp.where(odd == 1, other, 0.0)

        @pl.when(has_before)
        def _():
            to_after(h).wait_recv()

            @pl.when(has_after)
            def _():
                c_send[h] = (total + c_recv[h].astype(F32)).astype(BF16)

            carry[h] = (mine + c_recv[h].astype(F32)).astype(BF16)

        @pl.when(jnp.logical_not(has_before))
        def _():
            c_send[h] = total.astype(BF16)
            carry[h] = mine.astype(BF16)

        @pl.when(has_after)
        def _():
            to_after(h).start()

        @pl.when(h >= plain)
        def _():
            carry_across(h).start()

        attention = within[...] + dot(q[:, columns], carry[h])
        g[0, h] = normalize(attention, gain[:, columns])
        to_sibling(h).start()

        @pl.when(jnp.logical_and(h < AHEAD, h < plain))
        def _():
            to_across(h).start()

        return 0

    lax.fori_loop(0, heads, head_step, 0)

    def whole_slot(slot, fresh):
        for n in range(0, acc.shape[1], TILE):
            columns = slice(n, n + TILE)
            part = None if fresh else acc[:, columns]
            for h in range(0, heads, 2):
                lhs = jnp.concatenate([g[slot, h], g[slot, h + 1]], axis=1)
                new = dot(lhs, w[slot, h * DH : (h + 2) * DH, columns])
                part = new if part is None else part + new
            acc[:, columns] = part

    w_loads[0].wait()
    whole_slot(0, True)
    w_loads[1].wait()

    def sibling_step(h, _):
        to_sibling(h).wait_recv()
        return 0

    lax.fori_loop(0, heads, sibling_step, 0)
    whole_slot(1, False)
    w_loads[2].wait()
    w_loads[3].wait()

    gain_across().wait()

    def arrive(h):
        @pl.when(h >= plain)
        def _():
            q_across(h).wait_recv()
            within_across(h).wait_recv()
            carry_across(h).wait_recv()
            n = h - (heads - EARLY)
            attention = far_within[n].astype(F32) + dot(far_q[n], far_carry[n])
            g[2, h] = normalize(attention, far_gain[:, columns_of(h)])

        @pl.when(h < plain)
        def _():
            to_across(h).wait_recv()

        pass_on(h).start()

        @pl.when(h + AHEAD < plain)
        def _():
            to_across(h).wait_send()
            to_across(h + AHEAD).start()

    def rows_of(slot, h):
        return w[slot, columns_of(h)]

    def order(p):
        return lax.rem(p + plain, heads)

    start = order(0)
    arrive(start)
    acc[...] += dot(g[2, start], rows_of(2, start))

    def across_step(p, _):
        h, before = order(p), order(p - 1)
        arrive(h)
        pass_on(before).wait_recv()
        lhs = jnp.concatenate([g[2, h], g[3, before]], axis=1)
        rhs = jnp.concatenate([rows_of(2, h), rows_of(3, before)], axis=0)
        acc[...] += dot(lhs, rhs)
        return 0

    lax.fori_loop(1, heads, across_step, 0)
    final = order(heads - 1)
    pass_on(final).wait_recv()
    for n in range(0, acc.shape[1], TILE):
        columns = slice(n, n + TILE)
        last = dot(g[3, final], w[3, columns_of(final), columns])
        o_ref[:, columns] = (acc[:, columns] + last).astype(BF16)

    def drain(h, _):
        to_pair(h).wait_send()
        to_sibling(h).wait_send()
        pass_on(h).wait_send()

        @pl.when(jnp.logical_and(h < plain, h + AHEAD >= plain))
        def _():
            to_across(h).wait_send()

        @pl.when(h >= plain)
        def _():
            q_across(h).wait_send()
            within_across(h).wait_send()
            carry_across(h).wait_send()

        @pl.when(has_after)
        def _():
            to_after(h).wait_send()

        return 0

    lax.fori_loop(0, heads, drain, 0)


def shards(seq_n, query_rows, key_rows, value_rows, norm_gain, out_weight):
    tokens, width = query_rows.shape
    heads = width // DH
    features = out_weight.shape[1]
    hbm = pl.BlockSpec(memory_space=pltpu.HBM)
    vmem = pl.BlockSpec(memory_space=pltpu.VMEM)
    small = (heads, DH, DH)
    return pl.pallas_call(
        functools.partial(kernel, seq_n),
        out_shape=jax.ShapeDtypeStruct((tokens, features), BF16),
        in_specs=[hbm] * 5,
        out_specs=vmem,
        scratch_shapes=[
            pltpu.VMEM((tokens, width), BF16),
            pltpu.VMEM((tokens, width), BF16),
            pltpu.VMEM((tokens, width), BF16),
            pltpu.VMEM((4, width, features), BF16),
            pltpu.VMEM((4, heads, tokens, DH), BF16),
            pltpu.VMEM(small, F32),
            pltpu.VMEM(small, BF16),
            pltpu.VMEM(small, BF16),
            pltpu.VMEM(small, BF16),
            pltpu.VMEM(small, BF16),
            pltpu.VMEM(small, BF16),
            pltpu.VMEM((tokens, DH), F32),
            pltpu.VMEM((tokens, features), F32),
            pltpu.VMEM((1, width), F32),
            pltpu.VMEM((1, width), F32),
            pltpu.VMEM((EARLY, tokens, DH), BF16),
            pltpu.VMEM((EARLY, tokens, DH), BF16),
            pltpu.VMEM((EARLY, DH, DH), BF16),
            pltpu.VMEM((EARLY, tokens, DH), BF16),
            pltpu.SemaphoreType.DMA((6,)),
            pltpu.SemaphoreType.DMA((4,)),
            pltpu.SemaphoreType.DMA((2,)),
        ]
        + [pltpu.SemaphoreType.DMA((heads,))] * 10
        + [pltpu.SemaphoreType.DMA((EARLY,))] * 4,
        compiler_params=pltpu.CompilerParams(
            collective_id=0, has_side_effects=True, vmem_limit_bytes=62 * 1024 * 1024
        ),
        cost_estimate=pl.CostEstimate(
            flops=2 * tokens * width * 4 * features + 6 * tokens * tokens * width,
            bytes_accessed=2 * (4 * tokens * width + 4 * width * features),
            transcendentals=tokens * heads,
        ),
    )(query_rows, key_rows, value_rows, norm_gain.reshape(1, -1), out_weight)


def solution(mesh):
    placed = (P("seq", "fsdp"), P("seq", "fsdp"), P("seq", "fsdp"), P("fsdp"), P(None, "fsdp"))
    return jax.shard_map(
        functools.partial(shards, mesh.shape["seq"]),
        mesh=mesh, in_specs=placed, out_specs=P("seq", "fsdp"), check_vma=False,
    )
```

```python
import functools

import jax
import jax.numpy as jnp
from jax import lax
from jax.experimental import pallas as pl
from jax.experimental.pallas import tpu as pltpu
from jax.sharding import PartitionSpec as P

DH = 128
TILE = 256
AHEAD = 4
EARLY = 2
MESH = pl.DeviceIdType.MESH
F32 = jnp.float32
BF16 = jnp.bfloat16


def dot(a, b, contract=((1,), (0,))):
    return lax.dot_general(a, b, (contract, ((), ())), preferred_element_type=F32)


def kernel(
    seq_n, q_hbm, k_hbm, v_hbm, gain_hbm, w_hbm, o_ref,
    q, k, v, w, g, state, s_send, x_recv, c_send, c_recv, carry, within, acc,
    gain, far_gain, far_q, far_within, far_carry, within_send,
    load_sem, w_sem, gain_sem, xs, xr, cs, cr, ss, sr, ys, yr, fs, fr, qs, qr, ws, wr,
):
    tokens, width = q.shape
    heads = width // DH
    i, f = lax.axis_index("seq"), lax.axis_index("fsdp")
    odd = lax.rem(i, 2)
    pair = i + 1 - 2 * odd
    sibling = f + 1 - 2 * lax.rem(f, 2)
    across = lax.rem(f + 2, 4)
    has_before = i >= 2
    has_after = i < seq_n - 2

    early = jnp.minimum(i // 2, min(EARLY, heads // 2))
    first, rest = pl.ds(0, 2 * DH), pl.ds(2 * DH, width - 2 * DH)
    pieces = (
        (k_hbm.at[:, first], k.at[:, first]), (v_hbm.at[:, first], v.at[:, first]),
        (k_hbm.at[:, rest], k.at[:, rest]), (v_hbm.at[:, rest], v.at[:, rest]),
        (q_hbm, q), (gain_hbm, gain),
    )
    loads = [pltpu.make_async_copy(src, dst, load_sem.at[n]) for n, (src, dst) in enumerate(pieces)]
    for load in loads:
        load.start()
    w_loads = []
    for slot, source in enumerate((f, sibling, across, 3 - f)):
        rows = pl.ds(pl.multiple_of(source * width, width), width)
        w_loads.append(pltpu.make_async_copy(w_hbm.at[rows], w.at[slot], w_sem.at[slot]))

    barrier = pltpu.get_barrier_semaphore()

    def greet(j, e):
        pl.semaphore_signal(barrier, inc=1, device_id=(j, e), device_id_type=MESH)

    greet(pair, f)
    greet(i, sibling)
    greet(i, across)

    @pl.when(has_before)
    def _():
        greet(i - 2, f)

    @pl.when(has_after)
    def _():
        greet(i + 2, f)

    pl.semaphore_wait(barrier, 3 + has_before.astype(jnp.int32) + has_after.astype(jnp.int32))

    def remote(src, dst, send, recv, h, where):
        return pltpu.make_async_remote_copy(
            src_ref=src.at[h], dst_ref=dst.at[h], send_sem=send.at[h], recv_sem=recv.at[h],
            device_id=where, device_id_type=MESH,
        )

    after = lax.rem(i + 2, seq_n)
    to_pair = lambda h: remote(s_send, x_recv, xs, xr, h, (pair, f))
    to_after = lambda h: remote(c_send, c_recv, cs, cr, h, (after, f))
    to_sibling = lambda h: remote(g.at[0], g.at[1], ss, sr, h, (i, sibling))
    to_across = lambda h: remote(g.at[0], g.at[2], ys, yr, h, (i, across))
    pass_on = lambda h: remote(g.at[2], g.at[3], fs, fr, h, (i, sibling))

    far = (i, across)

    def across_copy(src, dst, send, recv):
        return pltpu.make_async_remote_copy(
            src_ref=src, dst_ref=dst, send_sem=send, recv_sem=recv, device_id=far, device_id_type=MESH
        )

    def columns_of(h):
        return pl.ds(pl.multiple_of(h * DH, DH), DH)

    gain_across = lambda: across_copy(gain_hbm, far_gain, gain_sem.at[0], gain_sem.at[1])

    def q_across(h):
        return across_copy(q_hbm.at[:, columns_of(h)], far_q.at[h], qs.at[h], qr.at[h])

    def within_across(h):
        return across_copy(within_send.at[h], far_within.at[h], ws.at[h], wr.at[h])

    def carry_across(h):
        return across_copy(carry.at[h], far_carry.at[h], ys.at[h], yr.at[h])

    def start_early(h, _):
        q_across(h).start()
        return 0

    loads[0].wait()
    loads[1].wait()
    for h in range(heads):
        if h == 2:
            loads[2].wait()
            loads[3].wait()
        columns = slice(h * DH, (h + 1) * DH)
        s = dot(k[:, columns], v[:, columns], ((0,), (0,)))
        state[h] = s
        s_send[h] = s.astype(BF16)
        to_pair(h).start()
    gain_across().start()
    lax.fori_loop(0, early, start_early, 0)
    for load in w_loads:
        load.start()
    loads[4].wait()
    loads[5].wait()

    def form_within(h):
        columns = columns_of(h)
        for r in range(tokens // TILE):
            rows = slice(r * TILE, (r + 1) * TILE)
            scores = dot(q[rows, columns], k[: (r + 1) * TILE, columns], ((1,), (1,)))
            row = lax.broadcasted_iota(jnp.int32, scores.shape, 0) + r * TILE
            column = lax.broadcasted_iota(jnp.int32, scores.shape, 1)
            masked = jnp.where(column <= row, scores, 0.0).astype(BF16)
            within[rows] = dot(masked, v[: (r + 1) * TILE, columns])

    def early_step(h, _):
        form_within(h)
        within_send[h] = within[...].astype(BF16)
        within_across(h).start()
        return 0

    lax.fori_loop(0, early, early_step, 0)

    def normalize(attention, gains):
        mean_square = jnp.mean(attention * attention, axis=-1, keepdims=True)
        return (attention * lax.rsqrt(mean_square + 1e-06) * gains).astype(BF16)

    def head_step(h, _):
        columns = columns_of(h)
        form_within(h)
        to_pair(h).wait_recv()
        other = x_recv[h].astype(F32)
        total = state[h] + other
        mine = jnp.where(odd == 1, other, 0.0)

        @pl.when(has_before)
        def _():
            to_after(h).wait_recv()

            @pl.when(has_after)
            def _():
                c_send[h] = (total + c_recv[h].astype(F32)).astype(BF16)

            carry[h] = (mine + c_recv[h].astype(F32)).astype(BF16)

        @pl.when(jnp.logical_not(has_before))
        def _():
            c_send[h] = total.astype(BF16)
            carry[h] = mine.astype(BF16)

        @pl.when(has_after)
        def _():
            to_after(h).start()

        @pl.when(h < early)
        def _():
            carry_across(h).start()

        attention = within[...] + dot(q[:, columns], carry[h])
        g[0, h] = normalize(attention, gain[:, columns])
        to_sibling(h).start()

        @pl.when(jnp.logical_and(h >= early, h < early + AHEAD))
        def _():
            to_across(h).start()

        return 0

    lax.fori_loop(0, heads, head_step, 0)

    def whole_slot(slot, fresh):
        for n in range(0, acc.shape[1], TILE):
            columns = slice(n, n + TILE)
            part = None if fresh else acc[:, columns]
            for h in range(0, heads, 2):
                lhs = jnp.concatenate([g[slot, h], g[slot, h + 1]], axis=1)
                new = dot(lhs, w[slot, h * DH : (h + 2) * DH, columns])
                part = new if part is None else part + new
            acc[:, columns] = part

    w_loads[0].wait()
    whole_slot(0, True)
    w_loads[1].wait()

    def sibling_step(h, _):
        to_sibling(h).wait_recv()
        return 0

    lax.fori_loop(0, heads, sibling_step, 0)
    whole_slot(1, False)
    w_loads[2].wait()
    w_loads[3].wait()

    gain_across().wait()

    def arrive(h):
        @pl.when(h < early)
        def _():
            q_across(h).wait_recv()
            within_across(h).wait_recv()
            carry_across(h).wait_recv()
            attention = far_within[h].astype(F32) + dot(far_q[h], far_carry[h])
            g[2, h] = normalize(attention, far_gain[:, columns_of(h)])

        @pl.when(h >= early)
        def _():
            to_across(h).wait_recv()

        pass_on(h).start()

        @pl.when(jnp.logical_and(h >= early, h + AHEAD < heads))
        def _():
            to_across(h).wait_send()
            to_across(h + AHEAD).start()

    def rows_of(slot, h):
        return w[slot, columns_of(h)]

    arrive(jnp.int32(0))
    acc[...] += dot(g[2, 0], w[2, :DH])

    def across_step(h, _):
        before = h - 1
        arrive(h)
        pass_on(before).wait_recv()
        lhs = jnp.concatenate([g[2, h], g[3, before]], axis=1)
        rhs = jnp.concatenate([rows_of(2, h), rows_of(3, before)], axis=0)
        acc[...] += dot(lhs, rhs)
        return 0

    lax.fori_loop(1, heads, across_step, 0)
    final = heads - 1
    pass_on(final).wait_recv()
    for n in range(0, acc.shape[1], TILE):
        columns = slice(n, n + TILE)
        last = dot(g[3, final], w[3, final * DH :, columns])
        o_ref[:, columns] = (acc[:, columns] + last).astype(BF16)

    def drain(h, _):
        to_pair(h).wait_send()
        to_sibling(h).wait_send()
        pass_on(h).wait_send()

        @pl.when(jnp.logical_and(h >= early, h + AHEAD >= heads))
        def _():
            to_across(h).wait_send()

        @pl.when(h < early)
        def _():
            q_across(h).wait_send()
            within_across(h).wait_send()
            carry_across(h).wait_send()

        @pl.when(has_after)
        def _():
            to_after(h).wait_send()

        return 0

    lax.fori_loop(0, heads, drain, 0)


def shards(seq_n, query_rows, key_rows, value_rows, norm_gain, out_weight):
    tokens, width = query_rows.shape
    heads = width // DH
    features = out_weight.shape[1]
    hbm = pl.BlockSpec(memory_space=pltpu.HBM)
    vmem = pl.BlockSpec(memory_space=pltpu.VMEM)
    small = (heads, DH, DH)
    return pl.pallas_call(
        functools.partial(kernel, seq_n),
        out_shape=jax.ShapeDtypeStruct((tokens, features), BF16),
        in_specs=[hbm] * 5,
        out_specs=vmem,
        scratch_shapes=[
            pltpu.VMEM((tokens, width), BF16),
            pltpu.VMEM((tokens, width), BF16),
            pltpu.VMEM((tokens, width), BF16),
            pltpu.VMEM((4, width, features), BF16),
            pltpu.VMEM((4, heads, tokens, DH), BF16),
            pltpu.VMEM(small, F32),
            pltpu.VMEM(small, BF16),
            pltpu.VMEM(small, BF16),
            pltpu.VMEM(small, BF16),
            pltpu.VMEM(small, BF16),
            pltpu.VMEM(small, BF16),
            pltpu.VMEM((tokens, DH), F32),
            pltpu.VMEM((tokens, features), F32),
            pltpu.VMEM((1, width), F32),
            pltpu.VMEM((1, width), F32),
            pltpu.VMEM((EARLY, tokens, DH), BF16),
            pltpu.VMEM((EARLY, tokens, DH), BF16),
            pltpu.VMEM((EARLY, DH, DH), BF16),
            pltpu.VMEM((EARLY, tokens, DH), BF16),
            pltpu.SemaphoreType.DMA((6,)),
            pltpu.SemaphoreType.DMA((4,)),
            pltpu.SemaphoreType.DMA((2,)),
        ]
        + [pltpu.SemaphoreType.DMA((heads,))] * 10
        + [pltpu.SemaphoreType.DMA((EARLY,))] * 4,
        compiler_params=pltpu.CompilerParams(
            collective_id=0, has_side_effects=True, vmem_limit_bytes=52 * 1024 * 1024
        ),
        cost_estimate=pl.CostEstimate(
            flops=2 * tokens * width * 4 * features + 6 * tokens * tokens * width,
            bytes_accessed=2 * (4 * tokens * width + 4 * width * features),
            transcendentals=tokens * heads,
        ),
    )(query_rows, key_rows, value_rows, norm_gain.reshape(1, -1), out_weight)


def solution(mesh):
    placed = (P("seq", "fsdp"), P("seq", "fsdp"), P("seq", "fsdp"), P("fsdp"), P(None, "fsdp"))
    return jax.shard_map(
        functools.partial(shards, mesh.shape["seq"]),
        mesh=mesh, in_specs=placed, out_specs=P("seq", "fsdp"), check_vma=False,
    )
```

```python
import functools

import jax
import jax.numpy as jnp
from jax import lax
from jax.experimental import pallas as pl
from jax.experimental.pallas import tpu as pltpu
from jax.sharding import PartitionSpec as P

DH = 128
TILE = 256
AHEAD = 3
LEAD = 2
EARLY = 2
MESH = pl.DeviceIdType.MESH
F32 = jnp.float32
BF16 = jnp.bfloat16


def dot(a, b, contract=((1,), (0,))):
    return lax.dot_general(a, b, (contract, ((), ())), preferred_element_type=F32)


def kernel(
    seq_n, q_hbm, k_hbm, v_hbm, gain_hbm, w_hbm, o_ref,
    q, k, v, w, g, state, s_send, x_recv, c_send, c_recv, carry, within, acc,
    gain, far_gain, far_q, far_within, far_carry, within_send,
    load_sem, w_sem, gain_sem, xs, xr, cs, cr, ss, sr, ys, yr, fs, fr, qs, qr, ws, wr,
):
    tokens, width = q.shape
    heads = width // DH
    i, f = lax.axis_index("seq"), lax.axis_index("fsdp")
    odd = lax.rem(i, 2)
    pair = i + 1 - 2 * odd
    sibling = f + 1 - 2 * lax.rem(f, 2)
    across = lax.rem(f + 2, 4)
    has_before = i >= 2
    has_after = i < seq_n - 2

    early = jnp.clip(i // 2 - 1, 0, EARLY)

    def is_plain(h):
        return jnp.logical_or(h < LEAD, h >= LEAD + early)

    def follower(h):
        return h + AHEAD + jnp.where(h < LEAD, early, 0)

    first, rest = pl.ds(0, 2 * DH), pl.ds(2 * DH, width - 2 * DH)
    pieces = (
        (k_hbm.at[:, first], k.at[:, first]), (v_hbm.at[:, first], v.at[:, first]),
        (k_hbm.at[:, rest], k.at[:, rest]), (v_hbm.at[:, rest], v.at[:, rest]),
        (q_hbm, q), (gain_hbm, gain),
    )
    loads = [pltpu.make_async_copy(src, dst, load_sem.at[n]) for n, (src, dst) in enumerate(pieces)]
    for load in loads:
        load.start()
    w_loads = []
    for slot, source in enumerate((f, sibling, across, 3 - f)):
        rows = pl.ds(pl.multiple_of(source * width, width), width)
        w_loads.append(pltpu.make_async_copy(w_hbm.at[rows], w.at[slot], w_sem.at[slot]))

    barrier = pltpu.get_barrier_semaphore()

    def greet(j, e):
        pl.semaphore_signal(barrier, inc=1, device_id=(j, e), device_id_type=MESH)

    greet(pair, f)
    greet(i, sibling)
    greet(i, across)

    @pl.when(has_before)
    def _():
        greet(i - 2, f)

    @pl.when(has_after)
    def _():
        greet(i + 2, f)

    pl.semaphore_wait(barrier, 3 + has_before.astype(jnp.int32) + has_after.astype(jnp.int32))

    def remote(src, dst, send, recv, h, where):
        return pltpu.make_async_remote_copy(
            src_ref=src.at[h], dst_ref=dst.at[h], send_sem=send.at[h], recv_sem=recv.at[h],
            device_id=where, device_id_type=MESH,
        )

    after = lax.rem(i + 2, seq_n)
    to_pair = lambda h: remote(s_send, x_recv, xs, xr, h, (pair, f))
    to_after = lambda h: remote(c_send, c_recv, cs, cr, h, (after, f))
    to_sibling = lambda h: remote(g.at[0], g.at[1], ss, sr, h, (i, sibling))
    to_across = lambda h: remote(g.at[0], g.at[2], ys, yr, h, (i, across))
    pass_on = lambda h: remote(g.at[2], g.at[3], fs, fr, h, (i, sibling))

    far = (i, across)

    def across_copy(src, dst, send, recv):
        return pltpu.make_async_remote_copy(
            src_ref=src, dst_ref=dst, send_sem=send, recv_sem=recv, device_id=far, device_id_type=MESH
        )

    def columns_of(h):
        return pl.ds(pl.multiple_of(h * DH, DH), DH)

    gain_across = lambda: across_copy(gain_hbm, far_gain, gain_sem.at[0], gain_sem.at[1])

    def q_across(h):
        return across_copy(q_hbm.at[:, columns_of(h)], far_q.at[h - LEAD], qs.at[h - LEAD], qr.at[h - LEAD])

    def within_across(h):
        return across_copy(within_send.at[h - LEAD], far_within.at[h - LEAD], ws.at[h - LEAD], wr.at[h - LEAD])

    def carry_across(h):
        return across_copy(carry.at[h], far_carry.at[h - LEAD], ys.at[h], yr.at[h])

    def start_early(h, _):
        q_across(h).start()
        return 0

    loads[0].wait()
    loads[1].wait()
    for h in range(heads):
        if h == 2:
            loads[2].wait()
            loads[3].wait()
        columns = slice(h * DH, (h + 1) * DH)
        s = dot(k[:, columns], v[:, columns], ((0,), (0,)))
        state[h] = s
        s_send[h] = s.astype(BF16)
        to_pair(h).start()
    gain_across().start()
    lax.fori_loop(LEAD, LEAD + early, start_early, 0)
    for load in w_loads:
        load.start()
    loads[4].wait()
    loads[5].wait()

    def form_within(h):
        columns = columns_of(h)
        for r in range(tokens // TILE):
            rows = slice(r * TILE, (r + 1) * TILE)
            scores = dot(q[rows, columns], k[: (r + 1) * TILE, columns], ((1,), (1,)))
            row = lax.broadcasted_iota(jnp.int32, scores.shape, 0) + r * TILE
            column = lax.broadcasted_iota(jnp.int32, scores.shape, 1)
            masked = jnp.where(column <= row, scores, 0.0).astype(BF16)
            within[rows] = dot(masked, v[: (r + 1) * TILE, columns])

    def early_step(h, _):
        form_within(h)
        within_send[h - LEAD] = within[...].astype(BF16)
        within_across(h).start()
        return 0

    lax.fori_loop(LEAD, LEAD + early, early_step, 0)

    def normalize(attention, gains):
        mean_square = jnp.mean(attention * attention, axis=-1, keepdims=True)
        return (attention * lax.rsqrt(mean_square + 1e-06) * gains).astype(BF16)

    def head_step(h, _):
        columns = columns_of(h)
        form_within(h)
        to_pair(h).wait_recv()
        other = x_recv[h].astype(F32)
        total = state[h] + other
        mine = jnp.where(odd == 1, other, 0.0)

        @pl.when(has_before)
        def _():
            to_after(h).wait_recv()

            @pl.when(has_after)
            def _():
                c_send[h] = (total + c_recv[h].astype(F32)).astype(BF16)

            carry[h] = (mine + c_recv[h].astype(F32)).astype(BF16)

        @pl.when(jnp.logical_not(has_before))
        def _():
            c_send[h] = total.astype(BF16)
            carry[h] = mine.astype(BF16)

        @pl.when(has_after)
        def _():
            to_after(h).start()

        @pl.when(jnp.logical_not(is_plain(h)))
        def _():
            carry_across(h).start()

        attention = within[...] + dot(q[:, columns], carry[h])
        g[0, h] = normalize(attention, gain[:, columns])
        to_sibling(h).start()

        @pl.when(jnp.logical_and(is_plain(h), h < early + AHEAD))
        def _():
            to_across(h).start()

        return 0

    lax.fori_loop(0, heads, head_step, 0)

    def whole_slot(slot, fresh):
        for n in range(0, acc.shape[1], TILE):
            columns = slice(n, n + TILE)
            part = None if fresh else acc[:, columns]
            for h in range(0, heads, 2):
                lhs = jnp.concatenate([g[slot, h], g[slot, h + 1]], axis=1)
                new = dot(lhs, w[slot, h * DH : (h + 2) * DH, columns])
                part = new if part is None else part + new
            acc[:, columns] = part

    w_loads[0].wait()
    whole_slot(0, True)
    w_loads[1].wait()

    def sibling_step(h, _):
        to_sibling(h).wait_recv()
        return 0

    lax.fori_loop(0, heads, sibling_step, 0)
    whole_slot(1, False)
    w_loads[2].wait()
    w_loads[3].wait()

    gain_across().wait()

    def arrive(h):
        @pl.when(jnp.logical_not(is_plain(h)))
        def _():
            q_across(h).wait_recv()
            within_across(h).wait_recv()
            carry_across(h).wait_recv()
            attention = far_within[h - LEAD].astype(F32) + dot(far_q[h - LEAD], far_carry[h - LEAD])
            g[2, h] = normalize(attention, far_gain[:, columns_of(h)])

        @pl.when(is_plain(h))
        def _():
            to_across(h).wait_recv()

        pass_on(h).start()

        @pl.when(jnp.logical_and(is_plain(h), follower(h) < heads))
        def _():
            to_across(h).wait_send()
            to_across(follower(h)).start()

    def rows_of(slot, h):
        return w[slot, columns_of(h)]

    arrive(jnp.int32(0))
    acc[...] += dot(g[2, 0], w[2, :DH])

    def across_step(h, _):
        before = h - 1
        arrive(h)
        pass_on(before).wait_recv()
        lhs = jnp.concatenate([g[2, h], g[3, before]], axis=1)
        rhs = jnp.concatenate([rows_of(2, h), rows_of(3, before)], axis=0)
        acc[...] += dot(lhs, rhs)
        return 0

    lax.fori_loop(1, heads, across_step, 0)
    final = heads - 1
    pass_on(final).wait_recv()
    for n in range(0, acc.shape[1], TILE):
        columns = slice(n, n + TILE)
        last = dot(g[3, final], w[3, final * DH :, columns])
        o_ref[:, columns] = (acc[:, columns] + last).astype(BF16)

    def drain(h, _):
        to_pair(h).wait_send()
        to_sibling(h).wait_send()
        pass_on(h).wait_send()

        @pl.when(jnp.logical_and(is_plain(h), follower(h) >= heads))
        def _():
            to_across(h).wait_send()

        @pl.when(jnp.logical_not(is_plain(h)))
        def _():
            q_across(h).wait_send()
            within_across(h).wait_send()
            carry_across(h).wait_send()

        @pl.when(has_after)
        def _():
            to_after(h).wait_send()

        return 0

    lax.fori_loop(0, heads, drain, 0)


def shards(seq_n, query_rows, key_rows, value_rows, norm_gain, out_weight):
    tokens, width = query_rows.shape
    heads = width // DH
    features = out_weight.shape[1]
    hbm = pl.BlockSpec(memory_space=pltpu.HBM)
    vmem = pl.BlockSpec(memory_space=pltpu.VMEM)
    small = (heads, DH, DH)
    return pl.pallas_call(
        functools.partial(kernel, seq_n),
        out_shape=jax.ShapeDtypeStruct((tokens, features), BF16),
        in_specs=[hbm] * 5,
        out_specs=vmem,
        scratch_shapes=[
            pltpu.VMEM((tokens, width), BF16),
            pltpu.VMEM((tokens, width), BF16),
            pltpu.VMEM((tokens, width), BF16),
            pltpu.VMEM((4, width, features), BF16),
            pltpu.VMEM((4, heads, tokens, DH), BF16),
            pltpu.VMEM(small, F32),
            pltpu.VMEM(small, BF16),
            pltpu.VMEM(small, BF16),
            pltpu.VMEM(small, BF16),
            pltpu.VMEM(small, BF16),
            pltpu.VMEM(small, BF16),
            pltpu.VMEM((tokens, DH), F32),
            pltpu.VMEM((tokens, features), F32),
            pltpu.VMEM((1, width), F32),
            pltpu.VMEM((1, width), F32),
            pltpu.VMEM((EARLY, tokens, DH), BF16),
            pltpu.VMEM((EARLY, tokens, DH), BF16),
            pltpu.VMEM((EARLY, DH, DH), BF16),
            pltpu.VMEM((EARLY, tokens, DH), BF16),
            pltpu.SemaphoreType.DMA((6,)),
            pltpu.SemaphoreType.DMA((4,)),
            pltpu.SemaphoreType.DMA((2,)),
        ]
        + [pltpu.SemaphoreType.DMA((heads,))] * 10
        + [pltpu.SemaphoreType.DMA((EARLY,))] * 4,
        compiler_params=pltpu.CompilerParams(
            collective_id=0, has_side_effects=True, vmem_limit_bytes=52 * 1024 * 1024
        ),
        cost_estimate=pl.CostEstimate(
            flops=2 * tokens * width * 4 * features + 6 * tokens * tokens * width,
            bytes_accessed=2 * (4 * tokens * width + 4 * width * features),
            transcendentals=tokens * heads,
        ),
    )(query_rows, key_rows, value_rows, norm_gain.reshape(1, -1), out_weight)


def solution(mesh):
    placed = (P("seq", "fsdp"), P("seq", "fsdp"), P("seq", "fsdp"), P("fsdp"), P(None, "fsdp"))
    return jax.shard_map(
        functools.partial(shards, mesh.shape["seq"]),
        mesh=mesh, in_specs=placed, out_specs=P("seq", "fsdp"), check_vma=False,
    )
```

```python
import functools

import jax
import jax.numpy as jnp
from jax import lax
from jax.experimental import pallas as pl
from jax.experimental.pallas import tpu as pltpu
from jax.sharding import PartitionSpec as P

DH = 128
TILE = 256
AHEAD = 4
LEAD = 2
EARLY = 2
MESH = pl.DeviceIdType.MESH
F32 = jnp.float32
BF16 = jnp.bfloat16


def dot(a, b, contract=((1,), (0,))):
    return lax.dot_general(a, b, (contract, ((), ())), preferred_element_type=F32)


def kernel(
    seq_n, q_hbm, k_hbm, v_hbm, gain_hbm, w_hbm, o_ref,
    q, k, v, w, g, state, s_send, x_recv, c_send, c_recv, carry, within, acc,
    gain, far_gain, far_q, far_within, far_carry, within_send,
    load_sem, w_sem, gain_sem, xs, xr, cs, cr, ss, sr, ys, yr, fs, fr, qs, qr, ws, wr,
):
    tokens, width = q.shape
    heads = width // DH
    i, f = lax.axis_index("seq"), lax.axis_index("fsdp")
    odd = lax.rem(i, 2)
    pair = i + 1 - 2 * odd
    sibling = f + 1 - 2 * lax.rem(f, 2)
    across = lax.rem(f + 2, 4)
    has_before = i >= 2
    has_after = i < seq_n - 2

    early = jnp.clip(i // 2 - 1, 0, EARLY)

    def is_plain(h):
        return jnp.logical_or(h < LEAD, h >= LEAD + early)

    def follower(h):
        return h + AHEAD + jnp.where(h < LEAD, early, 0)

    first, rest = pl.ds(0, 2 * DH), pl.ds(2 * DH, width - 2 * DH)
    pieces = (
        (k_hbm.at[:, first], k.at[:, first]), (v_hbm.at[:, first], v.at[:, first]),
        (k_hbm.at[:, rest], k.at[:, rest]), (v_hbm.at[:, rest], v.at[:, rest]),
        (q_hbm, q), (gain_hbm, gain),
    )
    loads = [pltpu.make_async_copy(src, dst, load_sem.at[n]) for n, (src, dst) in enumerate(pieces)]
    for load in loads:
        load.start()
    w_loads = []
    for slot, source in enumerate((f, sibling, across, 3 - f)):
        rows = pl.ds(pl.multiple_of(source * width, width), width)
        w_loads.append(pltpu.make_async_copy(w_hbm.at[rows], w.at[slot], w_sem.at[slot]))

    barrier = pltpu.get_barrier_semaphore()

    def greet(j, e):
        pl.semaphore_signal(barrier, inc=1, device_id=(j, e), device_id_type=MESH)

    greet(pair, f)
    greet(i, sibling)
    greet(i, across)

    @pl.when(has_before)
    def _():
        greet(i - 2, f)

    @pl.when(has_after)
    def _():
        greet(i + 2, f)

    pl.semaphore_wait(barrier, 3 + has_before.astype(jnp.int32) + has_after.astype(jnp.int32))

    def remote(src, dst, send, recv, h, where):
        return pltpu.make_async_remote_copy(
            src_ref=src.at[h], dst_ref=dst.at[h], send_sem=send.at[h], recv_sem=recv.at[h],
            device_id=where, device_id_type=MESH,
        )

    after = lax.rem(i + 2, seq_n)
    to_pair = lambda h: remote(s_send, x_recv, xs, xr, h, (pair, f))
    to_after = lambda h: remote(c_send, c_recv, cs, cr, h, (after, f))
    to_sibling = lambda h: remote(g.at[0], g.at[1], ss, sr, h, (i, sibling))
    to_across = lambda h: remote(g.at[0], g.at[2], ys, yr, h, (i, across))
    pass_on = lambda h: remote(g.at[2], g.at[3], fs, fr, h, (i, sibling))

    far = (i, across)

    def across_copy(src, dst, send, recv):
        return pltpu.make_async_remote_copy(
            src_ref=src, dst_ref=dst, send_sem=send, recv_sem=recv, device_id=far, device_id_type=MESH
        )

    def columns_of(h):
        return pl.ds(pl.multiple_of(h * DH, DH), DH)

    gain_across = lambda: across_copy(gain_hbm, far_gain, gain_sem.at[0], gain_sem.at[1])

    def q_across(h):
        return across_copy(q_hbm.at[:, columns_of(h)], far_q.at[h - LEAD], qs.at[h - LEAD], qr.at[h - LEAD])

    def within_across(h):
        return across_copy(within_send.at[h - LEAD], far_within.at[h - LEAD], ws.at[h - LEAD], wr.at[h - LEAD])

    def carry_across(h):
        return across_copy(carry.at[h], far_carry.at[h - LEAD], ys.at[h], yr.at[h])

    def start_early(h, _):
        q_across(h).start()
        return 0

    loads[0].wait()
    loads[1].wait()
    for h in range(heads):
        if h == 2:
            loads[2].wait()
            loads[3].wait()
        columns = slice(h * DH, (h + 1) * DH)
        s = dot(k[:, columns], v[:, columns], ((0,), (0,)))
        state[h] = s
        s_send[h] = s.astype(BF16)
        to_pair(h).start()
    gain_across().start()
    lax.fori_loop(LEAD, LEAD + early, start_early, 0)
    for load in w_loads:
        load.start()
    loads[4].wait()
    loads[5].wait()

    def form_within(h):
        columns = columns_of(h)
        for r in range(tokens // TILE):
            rows = slice(r * TILE, (r + 1) * TILE)
            scores = dot(q[rows, columns], k[: (r + 1) * TILE, columns], ((1,), (1,)))
            row = lax.broadcasted_iota(jnp.int32, scores.shape, 0) + r * TILE
            column = lax.broadcasted_iota(jnp.int32, scores.shape, 1)
            masked = jnp.where(column <= row, scores, 0.0).astype(BF16)
            within[rows] = dot(masked, v[: (r + 1) * TILE, columns])

    def early_step(h, _):
        form_within(h)
        within_send[h - LEAD] = within[...].astype(BF16)
        within_across(h).start()
        return 0

    lax.fori_loop(LEAD, LEAD + early, early_step, 0)

    def normalize(attention, gains):
        mean_square = jnp.mean(attention * attention, axis=-1, keepdims=True)
        return (attention * lax.rsqrt(mean_square + 1e-06) * gains).astype(BF16)

    def head_step(h, _):
        columns = columns_of(h)
        form_within(h)
        to_pair(h).wait_recv()
        other = x_recv[h].astype(F32)
        total = state[h] + other
        mine = jnp.where(odd == 1, other, 0.0)

        @pl.when(has_before)
        def _():
            to_after(h).wait_recv()

            @pl.when(has_after)
            def _():
                c_send[h] = (total + c_recv[h].astype(F32)).astype(BF16)

            carry[h] = (mine + c_recv[h].astype(F32)).astype(BF16)

        @pl.when(jnp.logical_not(has_before))
        def _():
            c_send[h] = total.astype(BF16)
            carry[h] = mine.astype(BF16)

        @pl.when(has_after)
        def _():
            to_after(h).start()

        @pl.when(jnp.logical_not(is_plain(h)))
        def _():
            carry_across(h).start()

        attention = within[...] + dot(q[:, columns], carry[h])
        g[0, h] = normalize(attention, gain[:, columns])
        to_sibling(h).start()

        @pl.when(jnp.logical_and(is_plain(h), h < early + AHEAD))
        def _():
            to_across(h).start()

        return 0

    lax.fori_loop(0, heads, head_step, 0)

    def whole_slot(slot, fresh):
        for n in range(0, acc.shape[1], TILE):
            columns = slice(n, n + TILE)
            part = None if fresh else acc[:, columns]
            for h in range(0, heads, 2):
                lhs = jnp.concatenate([g[slot, h], g[slot, h + 1]], axis=1)
                new = dot(lhs, w[slot, h * DH : (h + 2) * DH, columns])
                part = new if part is None else part + new
            acc[:, columns] = part

    w_loads[0].wait()
    whole_slot(0, True)
    w_loads[1].wait()

    def sibling_step(h, _):
        to_sibling(h).wait_recv()
        return 0

    lax.fori_loop(0, heads, sibling_step, 0)
    whole_slot(1, False)
    w_loads[2].wait()
    w_loads[3].wait()

    gain_across().wait()

    def arrive(h):
        @pl.when(jnp.logical_not(is_plain(h)))
        def _():
            q_across(h).wait_recv()
            within_across(h).wait_recv()
            carry_across(h).wait_recv()
            attention = far_within[h - LEAD].astype(F32) + dot(far_q[h - LEAD], far_carry[h - LEAD])
            g[2, h] = normalize(attention, far_gain[:, columns_of(h)])

        @pl.when(is_plain(h))
        def _():
            to_across(h).wait_recv()

        pass_on(h).start()

        @pl.when(jnp.logical_and(is_plain(h), follower(h) < heads))
        def _():
            to_across(h).wait_send()
            to_across(follower(h)).start()

    def rows_of(slot, h):
        return w[slot, columns_of(h)]

    arrive(jnp.int32(0))
    acc[...] += dot(g[2, 0], w[2, :DH])

    def across_step(h, _):
        before = h - 1
        arrive(h)
        pass_on(before).wait_recv()
        lhs = jnp.concatenate([g[2, h], g[3, before]], axis=1)
        rhs = jnp.concatenate([rows_of(2, h), rows_of(3, before)], axis=0)
        acc[...] += dot(lhs, rhs)
        return 0

    lax.fori_loop(1, heads, across_step, 0)
    final = heads - 1
    pass_on(final).wait_recv()
    for n in range(0, acc.shape[1], TILE):
        columns = slice(n, n + TILE)
        last = dot(g[3, final], w[3, final * DH :, columns])
        o_ref[:, columns] = (acc[:, columns] + last).astype(BF16)

    def drain(h, _):
        to_pair(h).wait_send()
        to_sibling(h).wait_send()
        pass_on(h).wait_send()

        @pl.when(jnp.logical_and(is_plain(h), follower(h) >= heads))
        def _():
            to_across(h).wait_send()

        @pl.when(jnp.logical_not(is_plain(h)))
        def _():
            q_across(h).wait_send()
            within_across(h).wait_send()
            carry_across(h).wait_send()

        @pl.when(has_after)
        def _():
            to_after(h).wait_send()

        return 0

    lax.fori_loop(0, heads, drain, 0)


def shards(seq_n, query_rows, key_rows, value_rows, norm_gain, out_weight):
    tokens, width = query_rows.shape
    heads = width // DH
    features = out_weight.shape[1]
    hbm = pl.BlockSpec(memory_space=pltpu.HBM)
    vmem = pl.BlockSpec(memory_space=pltpu.VMEM)
    small = (heads, DH, DH)
    return pl.pallas_call(
        functools.partial(kernel, seq_n),
        out_shape=jax.ShapeDtypeStruct((tokens, features), BF16),
        in_specs=[hbm] * 5,
        out_specs=vmem,
        scratch_shapes=[
            pltpu.VMEM((tokens, width), BF16),
            pltpu.VMEM((tokens, width), BF16),
            pltpu.VMEM((tokens, width), BF16),
            pltpu.VMEM((4, width, features), BF16),
            pltpu.VMEM((4, heads, tokens, DH), BF16),
            pltpu.VMEM(small, F32),
            pltpu.VMEM(small, BF16),
            pltpu.VMEM(small, BF16),
            pltpu.VMEM(small, BF16),
            pltpu.VMEM(small, BF16),
            pltpu.VMEM(small, BF16),
            pltpu.VMEM((tokens, DH), F32),
            pltpu.VMEM((tokens, features), F32),
            pltpu.VMEM((1, width), F32),
            pltpu.VMEM((1, width), F32),
            pltpu.VMEM((EARLY, tokens, DH), BF16),
            pltpu.VMEM((EARLY, tokens, DH), BF16),
            pltpu.VMEM((EARLY, DH, DH), BF16),
            pltpu.VMEM((EARLY, tokens, DH), BF16),
            pltpu.SemaphoreType.DMA((6,)),
            pltpu.SemaphoreType.DMA((4,)),
            pltpu.SemaphoreType.DMA((2,)),
        ]
        + [pltpu.SemaphoreType.DMA((heads,))] * 10
        + [pltpu.SemaphoreType.DMA((EARLY,))] * 4,
        compiler_params=pltpu.CompilerParams(
            collective_id=0, has_side_effects=True, vmem_limit_bytes=52 * 1024 * 1024
        ),
        cost_estimate=pl.CostEstimate(
            flops=2 * tokens * width * 4 * features + 6 * tokens * tokens * width,
            bytes_accessed=2 * (4 * tokens * width + 4 * width * features),
            transcendentals=tokens * heads,
        ),
    )(query_rows, key_rows, value_rows, norm_gain.reshape(1, -1), out_weight)


def solution(mesh):
    placed = (P("seq", "fsdp"), P("seq", "fsdp"), P("seq", "fsdp"), P("fsdp"), P(None, "fsdp"))
    return jax.shard_map(
        functools.partial(shards, mesh.shape["seq"]),
        mesh=mesh, in_specs=placed, out_specs=P("seq", "fsdp"), check_vma=False,
    )
```
